512 devices in a mesh: rep: 2 (over y_hi), row: 16 (over z, core), col: 16 (over x, y_lo).
Axes of the slice: x: 4, y: 8 (y_hi: 2, y_lo: 4; y = y_hi * 4 + y_lo), z: 8, core: 2. Of those that a mesh axis runs over, the one named last changes fastest.
Arguments:
- inputs: bfloat16 [512, 12288], P(('rep', 'col'), 'row'), may hold values from -6 to 6
- out_grad: bfloat16 [512, 12288], P(('rep', 'col'), 'row'), may hold values from -6 to 6
- w_in: bfloat16 [12288, 24576], P('row', ('rep', 'col')), may hold values from -0.0546875 to 0.0546875
- w_out: bfloat16 [24576, 12288], P(('rep', 'col'), 'row'), may hold values from -0.0390625 to 0.0390625
Outputs:
- grad_inputs: bfloat16 [512, 12288], P(('rep', 'col'), 'row')
- grad_w_in: bfloat16 [12288, 24576], P('row', ('rep', 'col'))
- grad_w_out: bfloat16 [24576, 12288], P(('rep', 'col'), 'row')
The draws below stay inside these ranges and needn't reach their ends.
All inputs are finite; a program needn't handle non-finite values.
Results may differ from the reference program's by a relative error of at most 0.005.
Values may be sent and summed in bfloat16 or wider, within the bound.
No kernel may reach another device: no remote copies, remote signals or barrier semaphores. Data moves between devices by JAX's collectives and lax.ppermute only.
A program may use at most 64 MiB of HBM per device.

```python
import jax
import jax.numpy as jnp
from jax import lax

D = 12288
FF = 24576
TOKENS = 512
FEAT_DEV = 768
HID_DEV = 768


def level_of(own_key, extent, split, least, high):
    def one(dim, blocks):
        heights = jax.random.uniform(jax.random.fold_in(jax.random.fold_in(own_key, 6), dim), (blocks,), jnp.float32, least / len(split), high / len(split))
        return jnp.repeat(jnp.exp(heights), extent[dim] // blocks).reshape((-1,) + (1,) * (len(extent) - dim - 1))

    loudness = one(*split[0])
    for cut in split[1:]:
        loudness = loudness * one(*cut)
    return loudness


def noise(rng, dims, scale, reach, cuts=(), dtype=jnp.bfloat16):
    values = scale * jax.random.normal(rng, dims, jnp.float32)
    if cuts:
        values = values * level_of(rng, dims, cuts, -0.22, 0.18)
    return jnp.clip(values, -reach, reach).astype(dtype)


def setup_inputs(seed: int = 0) -> dict:
    key_list = jax.random.split(jax.random.key(seed), 5)
    inputs = noise(key_list[0], (TOKENS, D), 1.0, 6.0, ((0, 32), (1, 16)))
    out_grad = noise(key_list[1], (TOKENS, D), 1.0, 6.0, ((0, 32), (1, 16)))
    w_in = noise(key_list[2], (D, FF), D ** -0.5, 0.0546875, ((0, 16), (1, 32)))
    w_out = noise(key_list[3], (FF, D), FF ** -0.5, 0.0390625, ((0, 32), (1, 16)))
    return dict(inputs=inputs, out_grad=out_grad, w_in=w_in, w_out=w_out)


def gelu_tanh(value):
    return jax.nn.gelu(value, approximate=True)

def reference(inputs, out_grad, w_in, w_out):
    feat_blocks = D // FEAT_DEV
    in_blocks = inputs.reshape(TOKENS, feat_blocks, FEAT_DEV).transpose(1, 0, 2)
    grad_blocks = out_grad.reshape(TOKENS, feat_blocks, FEAT_DEV).transpose(1, 0, 2)
    win_blocks = w_in.reshape(feat_blocks, FEAT_DEV, FF)
    wout_blocks = w_out.reshape(FF, feat_blocks, FEAT_DEV).transpose(1, 0, 2)

    def add_block(carry, parts):
        in_part, grad_part, win_part, wout_part = parts
        first_term = jnp.dot(in_part, win_part, preferred_element_type=jnp.float32)
        second_term = jnp.dot(grad_part, wout_part.T, preferred_element_type=jnp.float32)
        return ((carry[0] + first_term, carry[1] + second_term), None)
    empty = jnp.zeros((TOKENS, FF), jnp.float32)
    (pre_act, back_grad), _ = lax.scan(add_block, (empty, empty), (in_blocks, grad_blocks, win_blocks, wout_blocks))
    act_value, pullback = jax.vjp(gelu_tanh, pre_act)
    activation = act_value.astype(jnp.bfloat16)
    pre_grad = pullback(back_grad)[0].astype(jnp.bfloat16)
    grad_w_in = jnp.dot(inputs.T, pre_grad, preferred_element_type=jnp.float32).astype(jnp.bfloat16)
    grad_w_out = jnp.dot(activation.T, out_grad, preferred_element_type=jnp.float32).astype(jnp.bfloat16)
    hid_blocks = FF // HID_DEV
    slope_blocks = pre_grad.reshape(TOKENS, hid_blocks, HID_DEV).transpose(1, 0, 2)
    column_blocks = w_in.reshape(D, hid_blocks, HID_DEV).transpose(1, 0, 2)

    def add_hidden(carry, parts):
        slope_part, column_part = parts
        return (carry + jnp.dot(slope_part, column_part.T, preferred_element_type=jnp.float32), None)
    grad_sum, _ = lax.scan(add_hidden, jnp.zeros((TOKENS, D), jnp.float32), (slope_blocks, column_blocks))
    return (grad_sum.astype(jnp.bfloat16), grad_w_in, grad_w_out)
```

```python
import jax
import jax.numpy as jnp
from jax import lax
from jax.sharding import Mesh
from jax.sharding import PartitionSpec as P

PLANE = ("x", "y_hi", "y_lo")
SIDE = ("y_hi", "y_lo")
ROW = ("z", "core")
SWAP = [(0, 1), (1, 0)]


def gelu_tanh(value):
    return jax.nn.gelu(value, approximate=True)


def spread(block, axes, count):
    copies = jnp.broadcast_to(block[None], (count,) + block.shape)
    return lax.all_to_all(copies, axes, 0, 0, tiled=True)


def dot(left, right, dims, out=jnp.float32):
    return lax.dot_general(
        left, right, (dims, ((), ())), preferred_element_type=jnp.float32
    ).astype(out)


def body(inputs, out_grad, w_in, w_out):
    bf16, f32 = jnp.bfloat16, jnp.float32
    feat, hid = w_in.shape
    rows = inputs.shape[0]
    half = hid // 2
    core = lax.axis_index("core")
    mine, other = core * half, (1 - core) * half

    with jax.named_scope("gather_tokens"):
        by_y = spread(jnp.stack([inputs, out_grad]), SIDE, 8)
        by_y = by_y.transpose(1, 0, 2, 3).reshape(2, 8 * rows, feat)
        by_x = spread(by_y, "x", 4)
        tokens = 32 * rows
        all_in = by_x[:, 0].reshape(tokens, feat)
        all_grad = by_x[:, 1].reshape(tokens, feat)

    w_in_other = lax.dynamic_slice(w_in, (0, other), (feat, half))
    w_in_mine = lax.dynamic_slice(w_in, (0, mine), (feat, half))
    w_out_other = lax.dynamic_slice(w_out, (other, 0), (half, feat))
    w_out_mine = lax.dynamic_slice(w_out, (mine, 0), (half, feat))

    with jax.named_scope("chip_sum"):
        sent = jnp.stack(
            [
                dot(all_in, w_in_other, ((1,), (1 - 1,)), bf16),
                dot(all_grad, w_out_other, ((1,), (1,)), bf16),
            ]
        )
        got = lax.ppermute(sent, "core", SWAP)
        pre_chip = dot(all_in, w_in_mine, ((1,), (0,))) + got[0].astype(f32)
        back_chip = dot(all_grad, w_out_mine, ((1,), (1,))) + got[1].astype(f32)

    with jax.named_scope("row_sum"):
        share = tokens // 16
        parts = jnp.stack(
            [
                pre_chip.astype(bf16).reshape(16, share, half),
                back_chip.astype(bf16).reshape(16, share, half),
            ],
            axis=1,
        )
        parts = lax.all_to_all(parts, ROW, 0, 0, tiled=True)
        sums = parts.reshape(8, 2, 2, share, half).astype(f32).sum(axis=0)
        pre_act = jnp.concatenate([sums[0, 0], sums[1, 0]], axis=1)
        back_grad = jnp.concatenate([sums[0, 1], sums[1, 1]], axis=1)

    act_value, pullback = jax.vjp(gelu_tanh, pre_act)
    activation = act_value.astype(bf16)
    pre_grad = pullback(back_grad)[0].astype(bf16)

    pre_grad = lax.all_gather(pre_grad, ROW, axis=0, tiled=True)
    with jax.named_scope("token_sum"):
        terms = dot(pre_grad, w_in, ((1,), (1,)), bf16).reshape(32, rows, feat)
        terms = lax.all_to_all(terms, PLANE, 0, 0, tiled=True)
        grad_inputs = terms.astype(f32).sum(axis=0).astype(bf16)

    activation = lax.all_gather(activation, ROW, axis=0, tiled=True)
    grad_w_in = dot(all_in, pre_grad, ((0,), (0,)), bf16)
    grad_w_out = dot(activation, all_grad, ((0,), (0,)), bf16)
    return (grad_inputs, grad_w_in, grad_w_out)


def solution(mesh):
    fine = Mesh(mesh.devices.reshape(2, 8, 2, 4, 4), ("y_hi", "z", "core", "x", "y_lo"))
    plane = ("y_hi", "x", "y_lo")
    token_block, up_block, down_block = P(plane, ROW), P(ROW, plane), P(plane, ROW)
    return jax.shard_map(
        body,
        mesh=fine,
        in_specs=(token_block, token_block, up_block, down_block),
        out_specs=(token_block, up_block, down_block),
        check_vma=False,
    )
```

```python
import jax
import jax.numpy as jnp
from jax import lax
from jax.experimental import pallas as pl
from jax.experimental.pallas import tpu as pltpu
from jax.sharding import Mesh
from jax.sharding import PartitionSpec as P

PLANE = ("x", "y_hi", "y_lo")
SIDE = ("y_hi", "y_lo", "core")
ROW = ("z", "core")
SWAP = [(0, 1), (1, 0)]


def gelu_tanh(value):
    return jax.nn.gelu(value, approximate=True)


def dot(left, right, dims, out=jnp.float32):
    return lax.dot_general(
        left, right, (dims, ((), ())), preferred_element_type=jnp.float32
    ).astype(out)


def terms_kernel(core, tokens, w_in, w_in_swap, w_out, w_out_swap, terms):
    near, far = core[0], 1 - core[0]
    count = tokens.shape[0] * tokens.shape[3]

    def lhs(side, kind):
        return tokens[:, side, kind].reshape(count, tokens.shape[4])

    pre = dot(lhs(near, 0), w_in[...], ((1,), (0,)))
    pre += dot(lhs(far, 0), w_in_swap[...], ((1,), (0,)))
    back = dot(lhs(near, 1), w_out[...], ((1,), (1,)))
    back += dot(lhs(far, 1), w_out_swap[...], ((1,), (1,)))
    for kind, value in enumerate((pre, back)):
        terms[:, kind] = value.astype(terms.dtype).reshape(16, count // 16, value.shape[1])


def chip_terms(core, tokens, w_in, w_in_swap, w_out, w_out_swap):
    feat, hid = w_in.shape
    block = 256
    count = tokens.shape[0] * tokens.shape[3]
    up = pl.BlockSpec((feat, block), lambda j, core: (0, j))
    down = pl.BlockSpec((block, feat), lambda j, core: (j, 0))
    return pl.pallas_call(
        terms_kernel,
        grid_spec=pltpu.PrefetchScalarGridSpec(
            num_scalar_prefetch=1,
            grid=(hid // block,),
            in_specs=[
                pl.BlockSpec(tokens.shape, lambda j, core: (0,) * 5),
                up,
                up,
                down,
                down,
            ],
            out_specs=pl.BlockSpec((16, 2, count // 16, block), lambda j, core: (0, 0, 0, j)),
        ),
        out_shape=jax.ShapeDtypeStruct((16, 2, count // 16, hid), jnp.bfloat16),
        compiler_params=pltpu.CompilerParams(vmem_limit_bytes=32 * 1024 * 1024),
        cost_estimate=pl.CostEstimate(
            flops=8 * count * feat * hid, bytes_accessed=8 * feat * hid, transcendentals=0
        ),
        name="chip_terms",
    )(core, tokens, w_in, w_in_swap, w_out, w_out_swap)


def body(inputs, out_grad, w_in, w_out):
    bf16, f32 = jnp.bfloat16, jnp.float32
    feat, hid = w_in.shape
    rows = inputs.shape[0]
    part = rows // 2
    core = lax.axis_index("core")
    first = core == 0

    w_in_swap = lax.ppermute(w_in, "core", SWAP)
    w_out_swap = lax.ppermute(w_out, "core", SWAP)

    with jax.named_scope("gather_tokens"):
        own = jnp.stack([inputs, out_grad]).reshape(2, 2, part, feat).transpose(1, 0, 2, 3)
        own = jnp.broadcast_to(own[None], (8, 2, 2, part, feat)).reshape(16, 2, part, feat)
        by_y = lax.all_to_all(own, SIDE, 0, 0, tiled=True).reshape(8, 2, 2, part, feat)
        by_y = by_y.transpose(1, 2, 0, 3, 4).reshape(2, 2, 8 * part, feat)
        by_x = jnp.broadcast_to(by_y[None], (4,) + by_y.shape)
        by_x = lax.all_to_all(by_x, "x", 0, 0, tiled=True)
        near = lax.dynamic_index_in_dim(by_x, core, 1, False)
        far = lax.dynamic_index_in_dim(by_x, 1 - core, 1, False)

    with jax.named_scope("row_sum"):
        terms = chip_terms(core.reshape(1), by_x, w_in, w_in_swap, w_out, w_out_swap)
        terms = lax.all_to_all(terms, ROW, 0, 0, tiled=True)
        sums = terms.reshape(8, 2, 2, 2, part, hid).astype(f32).sum(axis=0)
        pre_act, back_grad = (
            sums[:, k].transpose(1, 0, 2, 3).reshape(2 * rows, hid) for k in (0, 1)
        )

    with jax.named_scope("swap_tokens"):
        swapped = lax.ppermute(far, "core", SWAP)

        def both_halves(near, far):
            near, far = near.reshape(32, part, feat), far.reshape(32, part, feat)
            halves = [jnp.where(first, near, far), jnp.where(first, far, near)]
            return jnp.stack(halves, axis=1).reshape(32 * rows, feat)

        all_in = both_halves(near[:, 0], swapped[:, 0])
        all_grad = both_halves(near[:, 1], swapped[:, 1])

    act_value, pullback = jax.vjp(gelu_tanh, pre_act)
    activation = act_value.astype(bf16)
    pre_grad = pullback(back_grad)[0].astype(bf16)
    pre_grad = lax.all_gather(pre_grad, ROW, axis=0, tiled=True)

    with jax.named_scope("token_sum"):
        terms = dot(pre_grad, w_in, ((1,), (1,)), bf16).reshape(32, rows, feat)
        terms, activation = lax.optimization_barrier((terms, activation))
        terms = lax.all_to_all(terms, PLANE, 0, 0, tiled=True)
        grad_inputs = terms.astype(f32).sum(axis=0).astype(bf16)

    activation = lax.all_gather(activation, ROW, axis=0, tiled=True)
    grad_w_in = dot(all_in, pre_grad, ((0,), (0,)), bf16)
    grad_w_out = dot(activation, all_grad, ((0,), (0,)), bf16)
    return (grad_inputs, grad_w_in, grad_w_out)


def solution(mesh):
    fine = Mesh(mesh.devices.reshape(2, 8, 2, 4, 4), ("y_hi", "z", "core", "x", "y_lo"))
    plane = ("y_hi", "x", "y_lo")
    token_block, up_block, down_block = P(plane, ROW), P(ROW, plane), P(plane, ROW)
    return jax.shard_map(
        body,
        mesh=fine,
        in_specs=(token_block, token_block, up_block, down_block),
        out_specs=(token_block, up_block, down_block),
        check_vma=False,
    )
```

```python
import jax
import jax.numpy as jnp
from jax import lax
from jax.experimental import pallas as pl
from jax.experimental.pallas import tpu as pltpu
from jax.sharding import Mesh
from jax.sharding import PartitionSpec as P

PLANE = ("x", "y_hi", "y_lo")
SIDE = ("y_hi", "y_lo", "core")
ROW = ("z", "core")
SWAP = [(0, 1), (1, 0)]
ROW_ORDER = [[2 * z + core for z in range(7, -1, -1) for core in (0, 1)]]


def gelu_tanh(value):
    return jax.nn.gelu(value, approximate=True)


def dot(left, right, dims, out=jnp.float32):
    return lax.dot_general(
        left, right, (dims, ((), ())), preferred_element_type=jnp.float32
    ).astype(out)


def terms_kernel(core, tokens, w_in, w_in_swap, w_out, w_out_swap, terms, up, down, sems):
    near, far = core[0], 1 - core[0]
    blocks, _, feat, block = up.shape
    count = tokens.shape[0] * tokens.shape[3]

    def fetches(j):
        span = pl.ds(j * block, block)
        pairs = (
            (w_in.at[:, span], up.at[j, 0]),
            (w_in_swap.at[:, span], up.at[j, 1]),
            (w_out.at[span, :], down.at[j, 0]),
            (w_out_swap.at[span, :], down.at[j, 1]),
        )
        return [
            pltpu.make_async_copy(source, target, sems.at[j, k])
            for k, (source, target) in enumerate(pairs)
        ]

    for j in range(blocks):
        for fetch in fetches(j):
            fetch.start()

    def lhs(side, kind):
        return tokens[:, side, kind].reshape(count, feat)

    for j in range(blocks):
        for fetch in fetches(j):
            fetch.wait()
        pre = dot(lhs(near, 0), up[j, 0], ((1,), (0,)))
        pre += dot(lhs(far, 0), up[j, 1], ((1,), (0,)))
        back = dot(lhs(near, 1), down[j, 0], ((1,), (1,)))
        back += dot(lhs(far, 1), down[j, 1], ((1,), (1,)))
        for kind, value in enumerate((pre, back)):
            terms[:, kind, :, pl.ds(j * block, block)] = value.astype(terms.dtype).reshape(
                16, count // 16, block
            )


def chip_terms(core, tokens, *weights):
    feat, hid = weights[0].shape
    weights = [pltpu.with_memory_space_constraint(w, pltpu.HBM) for w in weights]
    block = 256
    blocks = hid // block
    count = tokens.shape[0] * tokens.shape[3]
    far = pl.BlockSpec(memory_space=pltpu.HBM)
    near = pl.BlockSpec(memory_space=pltpu.VMEM)
    return pl.pallas_call(
        terms_kernel,
        in_specs=[pl.BlockSpec(memory_space=pltpu.SMEM), near, far, far, far, far],
        out_specs=near,
        out_shape=jax.ShapeDtypeStruct((16, 2, count // 16, hid), jnp.bfloat16),
        scratch_shapes=[
            pltpu.VMEM((blocks, 2, feat, block), jnp.bfloat16),
            pltpu.VMEM((blocks, 2, block, feat), jnp.bfloat16),
            pltpu.SemaphoreType.DMA((blocks, 4)),
        ],
        compiler_params=pltpu.CompilerParams(vmem_limit_bytes=32 * 1024 * 1024),
        cost_estimate=pl.CostEstimate(
            flops=8 * count * feat * hid, bytes_accessed=8 * feat * hid, transcendentals=0
        ),
        name="chip_terms",
    )(core, tokens, *weights)


def body(inputs, out_grad, w_in, w_out):
    bf16, f32 = jnp.bfloat16, jnp.float32
    feat, hid = w_in.shape
    rows = inputs.shape[0]
    part = rows // 2
    core = lax.axis_index("core")
    first = core == 0

    with jax.named_scope("gather_tokens"):
        halves = [x.reshape(2, part, feat) for x in (inputs, out_grad)]
        own = jnp.concatenate(halves, axis=1)[None]
        own = jnp.broadcast_to(own, (8, 2, rows, feat)).reshape(16, rows, feat)
        by_y = lax.all_to_all(own, SIDE, 0, 0, tiled=True)
        by_y, w_in_own, w_out_own = lax.optimization_barrier((by_y, w_in, w_out))
        by_y = by_y.reshape(8, 2, 2, part, feat)
        by_y = by_y.transpose(1, 2, 0, 3, 4).reshape(2, 2, 8 * part, feat)
        by_x = jnp.broadcast_to(by_y[None], (4,) + by_y.shape)
        by_x = lax.all_to_all(by_x, "x", 0, 0, tiled=True)
        w_in_swap = lax.ppermute(w_in_own, "core", SWAP)
        w_out_swap = lax.ppermute(w_out_own, "core", SWAP)
        near = lax.dynamic_index_in_dim(by_x, core, 1, False)
        far = lax.dynamic_index_in_dim(by_x, 1 - core, 1, False)

    with jax.named_scope("row_sum"):
        terms = chip_terms(core.reshape(1), by_x, w_in, w_in_swap, w_out, w_out_swap)
        terms = lax.all_to_all(terms, ROW, 0, 0, axis_index_groups=ROW_ORDER, tiled=True)

    with jax.named_scope("swap_tokens"):
        swapped = lax.ppermute(far, "core", SWAP)

        def both_halves(near, far):
            near, far = near.reshape(32, part, feat), far.reshape(32, part, feat)
            halves = [jnp.where(first, near, far), jnp.where(first, far, near)]
            return jnp.stack(halves, axis=1).reshape(32 * rows, feat)

        all_in = both_halves(near[:, 0], swapped[:, 0])
        all_grad = both_halves(near[:, 1], swapped[:, 1])

    sums, all_in, all_grad = lax.optimization_barrier((terms, all_in, all_grad))
    sums = sums.reshape(8, 2, 2, 2, part, hid).astype(f32).sum(axis=0)
    pre_act, back_grad = (
        sums[:, k].transpose(1, 0, 2, 3).reshape(2 * rows, hid) for k in (0, 1)
    )
    act_value, pullback = jax.vjp(gelu_tanh, pre_act)
    activation = act_value.astype(bf16)
    pre_grad = pullback(back_grad)[0].astype(bf16)
    pre_grad = lax.all_gather(pre_grad, ROW, axis_index_groups=ROW_ORDER, axis=0, tiled=True)

    with jax.named_scope("token_sum"):
        terms = dot(pre_grad, w_in, ((1,), (1,)), bf16).reshape(32, rows, feat)
        terms, activation = lax.optimization_barrier((terms, activation))
        terms = lax.all_to_all(terms, PLANE, 0, 0, tiled=True)
        grad_inputs = terms.astype(f32).sum(axis=0).astype(bf16)

    activation = lax.all_gather(activation, ROW, axis_index_groups=ROW_ORDER, axis=0, tiled=True)
    activation, pre_grad = lax.optimization_barrier((activation, pre_grad))
    grad_w_in = dot(all_in, pre_grad, ((0,), (0,)), bf16)
    grad_w_out = dot(activation, all_grad, ((0,), (0,)), bf16)
    return (grad_inputs, grad_w_in, grad_w_out)


def solution(mesh):
    fine = Mesh(mesh.devices.reshape(2, 8, 2, 4, 4), ("y_hi", "z", "core", "x", "y_lo"))
    plane = ("y_hi", "x", "y_lo")
    token_block, up_block, down_block = P(plane, ROW), P(ROW, plane), P(plane, ROW)
    return jax.shard_map(
        body,
        mesh=fine,
        in_specs=(token_block, token_block, up_block, down_block),
        out_specs=(token_block, up_block, down_block),
        check_vma=False,
    )
```

```python
import jax
import jax.numpy as jnp
from jax import lax
from jax.experimental import pallas as pl
from jax.experimental.pallas import tpu as pltpu
from jax.sharding import Mesh
from jax.sharding import PartitionSpec as P

PLANE = ("x", "y_hi", "y_lo")
SIDE = ("y_hi", "y_lo", "core")
ROW = ("z", "core")
SWAP = [(0, 1), (1, 0)]
SIDE_ORDER = [[2 * y + core for y in range(7, -1, -1) for core in (0, 1)]]
PLANE_ORDER = [[8 * x + y for x in range(3, -1, -1) for y in range(7, -1, -1)]]
ROW_ORDER = [[2 * z + core for z in range(7, -1, -1) for core in (0, 1)]]


def gelu_tanh(value):
    return jax.nn.gelu(value, approximate=True)


def dot(left, right, dims, out=jnp.float32):
    return lax.dot_general(
        left, right, (dims, ((), ())), preferred_element_type=jnp.float32
    ).astype(out)


def terms_kernel(core, tokens, w_in, w_in_swap, w_out, w_out_swap, terms, up, down, sems):
    near, far = core[0], 1 - core[0]
    blocks, _, feat, block = up.shape
    count = tokens.shape[0] * tokens.shape[3]

    def fetches(j):
        span = pl.ds(j * block, block)
        pairs = (
            (w_in.at[:, span], up.at[j, 0]),
            (w_in_swap.at[:, span], up.at[j, 1]),
            (w_out.at[span, :], down.at[j, 0]),
            (w_out_swap.at[span, :], down.at[j, 1]),
        )
        return [
            pltpu.make_async_copy(source, target, sems.at[j, k])
            for k, (source, target) in enumerate(pairs)
        ]

    for j in range(blocks):
        for fetch in fetches(j):
            fetch.start()

    def lhs(side, kind):
        return tokens[:, side, kind].reshape(count, feat)

    for j in range(blocks):
        for fetch in fetches(j):
            fetch.wait()
        pre = dot(lhs(near, 0), up[j, 0], ((1,), (0,)))
        pre += dot(lhs(far, 0), up[j, 1], ((1,), (0,)))
        back = dot(lhs(near, 1), down[j, 0], ((1,), (1,)))
        back += dot(lhs(far, 1), down[j, 1], ((1,), (1,)))
        for kind, value in enumerate((pre, back)):
            terms[:, kind, :, pl.ds(j * block, block)] = value.astype(terms.dtype).reshape(
                16, count // 16, block
            )


def chip_terms(core, tokens, *weights):
    feat, hid = weights[0].shape
    weights = [pltpu.with_memory_space_constraint(w, pltpu.HBM) for w in weights]
    block = 256
    blocks = hid // block
    count = tokens.shape[0] * tokens.shape[3]
    far = pl.BlockSpec(memory_space=pltpu.HBM)
    near = pl.BlockSpec(memory_space=pltpu.VMEM)
    return pl.pallas_call(
        terms_kernel,
        in_specs=[pl.BlockSpec(memory_space=pltpu.SMEM), near, far, far, far, far],
        out_specs=near,
        out_shape=jax.ShapeDtypeStruct((16, 2, count // 16, hid), jnp.bfloat16),
        scratch_shapes=[
            pltpu.VMEM((blocks, 2, feat, block), jnp.bfloat16),
            pltpu.VMEM((blocks, 2, block, feat), jnp.bfloat16),
            pltpu.SemaphoreType.DMA((blocks, 4)),
        ],
        compiler_params=pltpu.CompilerParams(vmem_limit_bytes=32 * 1024 * 1024),
        cost_estimate=pl.CostEstimate(
            flops=8 * count * feat * hid, bytes_accessed=8 * feat * hid, transcendentals=0
        ),
        name="chip_terms",
    )(core, tokens, *weights)


def body(inputs, out_grad, w_in, w_out):
    bf16, f32 = jnp.bfloat16, jnp.float32
    feat, hid = w_in.shape
    rows = inputs.shape[0]
    part = rows // 2
    core = lax.axis_index("core")
    first = core == 0

    with jax.named_scope("gather_tokens"):
        halves = [x.reshape(2, part, feat) for x in (inputs, out_grad)]
        own = jnp.concatenate(halves, axis=1)[None]
        own = jnp.broadcast_to(own, (8, 2, rows, feat)).reshape(16, rows, feat)
        by_y = lax.all_to_all(own, SIDE, 0, 0, axis_index_groups=SIDE_ORDER, tiled=True)
        by_y, w_in_own, w_out_own = lax.optimization_barrier((by_y, w_in, w_out))
        by_y = by_y.reshape(8, 2, 2, part, feat)
        by_y = by_y.transpose(1, 2, 0, 3, 4).reshape(2, 2, 8 * part, feat)
        by_x = jnp.broadcast_to(by_y[None], (4,) + by_y.shape)
        by_x = lax.all_to_all(
            by_x, "x", 0, 0, axis_index_groups=[[3, 2, 1, 0]], tiled=True
        )
        w_in_swap = lax.ppermute(w_in_own, "core", SWAP)
        w_out_swap = lax.ppermute(w_out_own, "core", SWAP)
        near = lax.dynamic_index_in_dim(by_x, core, 1, False)
        far = lax.dynamic_index_in_dim(by_x, 1 - core, 1, False)

    with jax.named_scope("row_sum"):
        terms = chip_terms(core.reshape(1), by_x, w_in, w_in_swap, w_out, w_out_swap)
        terms = lax.all_to_all(terms, ROW, 0, 0, axis_index_groups=ROW_ORDER, tiled=True)

    with jax.named_scope("swap_tokens"):
        swapped = lax.ppermute(far, "core", SWAP)

        def both_halves(near, far):
            near, far = near.reshape(32, part, feat), far.reshape(32, part, feat)
            halves = [jnp.where(first, near, far), jnp.where(first, far, near)]
            return jnp.stack(halves, axis=1).reshape(32 * rows, feat)

        all_in = both_halves(near[:, 0], swapped[:, 0])
        all_grad = both_halves(near[:, 1], swapped[:, 1])

    sums, all_in, all_grad = lax.optimization_barrier((terms, all_in, all_grad))
    sums = sums.reshape(8, 2, 2, 2, part, hid).astype(f32).sum(axis=0)
    pre_act, back_grad = (
        sums[:, k].transpose(1, 0, 2, 3).reshape(2 * rows, hid) for k in (0, 1)
    )
    act_value, pullback = jax.vjp(gelu_tanh, pre_act)
    activation = act_value.astype(bf16)
    pre_grad = pullback(back_grad)[0].astype(bf16)
    pre_grad = lax.all_gather(pre_grad, ROW, axis_index_groups=ROW_ORDER, axis=0, tiled=True)

    with jax.named_scope("token_sum"):
        terms = dot(pre_grad, w_in, ((1,), (1,)), bf16).reshape(32, rows, feat)
        terms, activation = lax.optimization_barrier((terms, activation))
        terms = lax.all_to_all(
            terms, PLANE, 0, 0, axis_index_groups=PLANE_ORDER, tiled=True
        )
        grad_inputs = terms.astype(f32).sum(axis=0).astype(bf16)

    activation = lax.all_gather(activation, ROW, axis_index_groups=ROW_ORDER, axis=0, tiled=True)
    activation, pre_grad = lax.optimization_barrier((activation, pre_grad))
    grad_w_in = dot(all_in, pre_grad, ((0,), (0,)), bf16)
    grad_w_out = dot(activation, all_grad, ((0,), (0,)), bf16)
    return (grad_inputs, grad_w_in, grad_w_out)


def solution(mesh):
    fine = Mesh(mesh.devices.reshape(2, 8, 2, 4, 4), ("y_hi", "z", "core", "x", "y_lo"))
    plane = ("y_hi", "x", "y_lo")
    token_block, up_block, down_block = P(plane, ROW), P(ROW, plane), P(plane, ROW)
    return jax.shard_map(
        body,
        mesh=fine,
        in_specs=(token_block, token_block, up_block, down_block),
        out_specs=(token_block, up_block, down_block),
        check_vma=False,
    )
```

```python
import jax
import jax.numpy as jnp
from jax import lax
from jax.experimental import pallas as pl
from jax.experimental.pallas import tpu as pltpu
from jax.sharding import Mesh
from jax.sharding import PartitionSpec as P

PLANE = ("x", "y_hi", "y_lo")
SIDE = ("y_hi", "y_lo", "core")
ROW = ("z", "core")
SWAP = [(0, 1), (1, 0)]
SIDE_ORDER = [[2 * y + core for y in range(7, -1, -1) for core in (0, 1)]]
ROW_ORDER = [[2 * z + core for z in range(7, -1, -1) for core in (0, 1)]]


def gelu_tanh(value):
    return jax.nn.gelu(value, approximate=True)


def dot(left, right, dims, out=jnp.float32):
    return lax.dot_general(
        left, right, (dims, ((), ())), preferred_element_type=jnp.float32
    ).astype(out)


def terms_kernel(core, tokens, w_in, w_in_swap, w_out, w_out_swap, terms, up, down, sems):
    near, far = core[0], 1 - core[0]
    blocks, _, feat, block = up.shape
    count = tokens.shape[0] * tokens.shape[3]

    def fetches(j):
        span = pl.ds(j * block, block)
        pairs = (
            (w_in.at[:, span], up.at[j, 0]),
            (w_in_swap.at[:, span], up.at[j, 1]),
            (w_out.at[span, :], down.at[j, 0]),
            (w_out_swap.at[span, :], down.at[j, 1]),
        )
        return [
            pltpu.make_async_copy(source, target, sems.at[j, k])
            for k, (source, target) in enumerate(pairs)
        ]

    for j in range(blocks):
        for fetch in fetches(j):
            fetch.start()

    def lhs(side, kind):
        return tokens[:, side, kind].reshape(count, feat)

    for j in range(blocks):
        for fetch in fetches(j):
            fetch.wait()
        pre = dot(lhs(near, 0), up[j, 0], ((1,), (0,)))
        pre += dot(lhs(far, 0), up[j, 1], ((1,), (0,)))
        back = dot(lhs(near, 1), down[j, 0], ((1,), (1,)))
        back += dot(lhs(far, 1), down[j, 1], ((1,), (1,)))
        for kind, value in enumerate((pre, back)):
            terms[:, kind, :, pl.ds(j * block, block)] = value.astype(terms.dtype).reshape(
                16, count // 16, block
            )


def chip_terms(core, tokens, *weights):
    feat, hid = weights[0].shape
    weights = [pltpu.with_memory_space_constraint(w, pltpu.HBM) for w in weights]
    block = 256
    blocks = hid // block
    count = tokens.shape[0] * tokens.shape[3]
    far = pl.BlockSpec(memory_space=pltpu.HBM)
    near = pl.BlockSpec(memory_space=pltpu.VMEM)
    return pl.pallas_call(
        terms_kernel,
        in_specs=[pl.BlockSpec(memory_space=pltpu.SMEM), near, far, far, far, far],
        out_specs=near,
        out_shape=jax.ShapeDtypeStruct((16, 2, count // 16, hid), jnp.bfloat16),
        scratch_shapes=[
            pltpu.VMEM((blocks, 2, feat, block), jnp.bfloat16),
            pltpu.VMEM((blocks, 2, block, feat), jnp.bfloat16),
            pltpu.SemaphoreType.DMA((blocks, 4)),
        ],
        compiler_params=pltpu.CompilerParams(vmem_limit_bytes=32 * 1024 * 1024),
        cost_estimate=pl.CostEstimate(
            flops=8 * count * feat * hid, bytes_accessed=8 * feat * hid, transcendentals=0
        ),
        name="chip_terms",
    )(core, tokens, *weights)


def body(inputs, out_grad, w_in, w_out):
    bf16, f32 = jnp.bfloat16, jnp.float32
    feat, hid = w_in.shape
    rows = inputs.shape[0]
    part = rows // 2
    core = lax.axis_index("core")
    first = core == 0

    with jax.named_scope("gather_tokens"):
        halves = [x.reshape(2, part, feat) for x in (inputs, out_grad)]
        own = jnp.concatenate(halves, axis=1)[None]
        own = jnp.broadcast_to(own, (8, 2, rows, feat)).reshape(16, rows, feat)
        by_y = lax.all_to_all(own, SIDE, 0, 0, axis_index_groups=SIDE_ORDER, tiled=True)
        by_y, w_in_own, w_out_own = lax.optimization_barrier((by_y, w_in, w_out))
        by_y = by_y.reshape(8, 2, 2, part, feat)
        by_y = by_y[::-1].transpose(1, 2, 0, 3, 4).reshape(2, 2, 8 * part, feat)
        by_x = jnp.broadcast_to(by_y[None], (4,) + by_y.shape)
        by_x = lax.all_to_all(by_x, "x", 0, 0, tiled=True)
        w_in_swap = lax.ppermute(w_in_own, "core", SWAP)
        w_out_swap = lax.ppermute(w_out_own, "core", SWAP)
        near = lax.dynamic_index_in_dim(by_x, core, 1, False)
        far = lax.dynamic_index_in_dim(by_x, 1 - core, 1, False)

    with jax.named_scope("row_sum"):
        terms = chip_terms(core.reshape(1), by_x, w_in, w_in_swap, w_out, w_out_swap)
        terms = lax.all_to_all(terms, ROW, 0, 0, axis_index_groups=ROW_ORDER, tiled=True)

    with jax.named_scope("swap_tokens"):
        swapped = lax.ppermute(far, "core", SWAP)

        def both_halves(near, far):
            near, far = near.reshape(32, part, feat), far.reshape(32, part, feat)
            halves = [jnp.where(first, near, far), jnp.where(first, far, near)]
            return jnp.stack(halves, axis=1).reshape(32 * rows, feat)

        all_in = both_halves(near[:, 0], swapped[:, 0])
        all_grad = both_halves(near[:, 1], swapped[:, 1])

    sums, all_in, all_grad = lax.optimization_barrier((terms, all_in, all_grad))
    sums = sums.reshape(8, 2, 2, 2, part, hid).astype(f32).sum(axis=0)
    pre_act, back_grad = (
        sums[:, k].transpose(1, 0, 2, 3).reshape(2 * rows, hid) for k in (0, 1)
    )
    act_value, pullback = jax.vjp(gelu_tanh, pre_act)
    activation = act_value.astype(bf16)
    pre_grad = pullback(back_grad)[0].astype(bf16)
    pre_grad = lax.all_gather(pre_grad, ROW, axis_index_groups=ROW_ORDER, axis=0, tiled=True)

    with jax.named_scope("token_sum"):
        terms = dot(pre_grad, w_in, ((1,), (1,)), bf16).reshape(32, rows, feat)
        terms, activation = lax.optimization_barrier((terms, activation))
        terms = lax.all_to_all(terms, PLANE, 0, 0, tiled=True)
        grad_inputs = terms.astype(f32).sum(axis=0).astype(bf16)

    activation = lax.all_gather(activation, ROW, axis_index_groups=ROW_ORDER, axis=0, tiled=True)
    activation, pre_grad = lax.optimization_barrier((activation, pre_grad))
    grad_w_in = dot(all_in, pre_grad, ((0,), (0,)), bf16)
    grad_w_out = dot(activation, all_grad, ((0,), (0,)), bf16)
    return (grad_inputs, grad_w_in, grad_w_out)


def solution(mesh):
    fine = Mesh(mesh.devices.reshape(2, 8, 2, 4, 4), ("y_hi", "z", "core", "x", "y_lo"))
    plane = ("y_hi", "x", "y_lo")
    token_block, up_block, down_block = P(plane, ROW), P(ROW, plane), P(plane, ROW)
    return jax.shard_map(
        body,
        mesh=fine,
        in_specs=(token_block, token_block, up_block, down_block),
        out_specs=(token_block, up_block, down_block),
        check_vma=False,
    )
```

```python
import jax
import jax.numpy as jnp
from jax import lax
from jax.experimental import pallas as pl
from jax.experimental.pallas import tpu as pltpu
from jax.sharding import Mesh
from jax.sharding import PartitionSpec as P

PLANE = ("x", "y_hi", "y_lo")
SIDE = ("y_hi", "y_lo")
ROW = ("z", "core")
SWAP = [(0, 1), (1, 0)]
SIDE_ORDER = [list(range(7, -1, -1))]
ROW_ORDER = [[2 * z + core for z in range(7, -1, -1) for core in (0, 1)]]


def gelu_tanh(value):
    return jax.nn.gelu(value, approximate=True)


def dot(left, right, dims, out=jnp.float32):
    return lax.dot_general(
        left, right, (dims, ((), ())), preferred_element_type=jnp.float32
    ).astype(out)


def terms_kernel(core, tokens, w_in, w_in_swap, w_out, w_out_swap, terms, up, down, sems):
    near, far = core[0], 1 - core[0]
    blocks, _, feat, block = up.shape
    count = tokens.shape[0] * tokens.shape[3]

    def fetches(j):
        span = pl.ds(j * block, block)
        pairs = (
            (w_in.at[:, span], up.at[j, 0]),
            (w_in_swap.at[:, span], up.at[j, 1]),
            (w_out.at[span, :], down.at[j, 0]),
            (w_out_swap.at[span, :], down.at[j, 1]),
        )
        return [
            pltpu.make_async_copy(source, target, sems.at[j, k])
            for k, (source, target) in enumerate(pairs)
        ]

    for j in range(blocks):
        for fetch in fetches(j):
            fetch.start()

    def lhs(side, kind):
        return tokens[:, side, kind].reshape(count, feat)

    for j in range(blocks):
        for fetch in fetches(j):
            fetch.wait()
        pre = dot(lhs(near, 0), up[j, 0], ((1,), (0,)))
        pre += dot(lhs(far, 0), up[j, 1], ((1,), (0,)))
        back = dot(lhs(near, 1), down[j, 0], ((1,), (1,)))
        back += dot(lhs(far, 1), down[j, 1], ((1,), (1,)))
        for kind, value in enumerate((pre, back)):
            terms[:, kind, :, pl.ds(j * block, block)] = value.astype(terms.dtype).reshape(
                16, count // 16, block
            )


def chip_terms(core, tokens, *weights):
    feat, hid = weights[0].shape
    weights = [pltpu.with_memory_space_constraint(w, pltpu.HBM) for w in weights]
    block = 256
    blocks = hid // block
    count = tokens.shape[0] * tokens.shape[3]
    far = pl.BlockSpec(memory_space=pltpu.HBM)
    near = pl.BlockSpec(memory_space=pltpu.VMEM)
    return pl.pallas_call(
        terms_kernel,
        in_specs=[pl.BlockSpec(memory_space=pltpu.SMEM), near, far, far, far, far],
        out_specs=near,
        out_shape=jax.ShapeDtypeStruct((16, 2, count // 16, hid), jnp.bfloat16),
        scratch_shapes=[
            pltpu.VMEM((blocks, 2, feat, block), jnp.bfloat16),
            pltpu.VMEM((blocks, 2, block, feat), jnp.bfloat16),
            pltpu.SemaphoreType.DMA((blocks, 4)),
        ],
        compiler_params=pltpu.CompilerParams(vmem_limit_bytes=32 * 1024 * 1024),
        cost_estimate=pl.CostEstimate(
            flops=8 * count * feat * hid, bytes_accessed=8 * feat * hid, transcendentals=0
        ),
        name="chip_terms",
    )(core, tokens, *weights)


def body(inputs, out_grad, w_in, w_out):
    bf16, f32 = jnp.bfloat16, jnp.float32
    feat, hid = w_in.shape
    rows = inputs.shape[0]
    part = rows // 2
    core = lax.axis_index("core")
    first = core == 0

    with jax.named_scope("gather_tokens"):
        own = jnp.concatenate([inputs, out_grad])
        own = jnp.broadcast_to(own[None], (8,) + own.shape)
        by_y = lax.all_to_all(own, SIDE, 0, 0, axis_index_groups=SIDE_ORDER, tiled=True)
        by_y, w_in_own, w_out_own = lax.optimization_barrier((by_y, w_in, w_out))
        by_y = by_y.reshape(8, 2, 2, part, feat)
        by_y = by_y[::-1].transpose(2, 1, 0, 3, 4).reshape(2, 2, 8 * part, feat)
        by_x = jnp.broadcast_to(by_y[None], (4,) + by_y.shape)
        by_x = by_x.reshape(8, 2, 8 * part, feat)
        by_x = lax.all_to_all(by_x, ("x", "core"), 0, 0, tiled=True)
        by_x = by_x.reshape(4, 2, 2, 8 * part, feat)
        w_in_swap = lax.ppermute(w_in_own, "core", SWAP)
        w_out_swap = lax.ppermute(w_out_own, "core", SWAP)
        near = lax.dynamic_index_in_dim(by_x, core, 1, False)
        far = lax.dynamic_index_in_dim(by_x, 1 - core, 1, False)

    with jax.named_scope("row_sum"):
        terms = chip_terms(core.reshape(1), by_x, w_in, w_in_swap, w_out, w_out_swap)
        terms = lax.all_to_all(terms, ROW, 0, 0, axis_index_groups=ROW_ORDER, tiled=True)

    with jax.named_scope("swap_tokens"):
        swapped = lax.ppermute(far, "core", SWAP)

        def both_halves(near, far):
            near, far = near.reshape(32, part, feat), far.reshape(32, part, feat)
            halves = [jnp.where(first, near, far), jnp.where(first, far, near)]
            return jnp.stack(halves, axis=1).reshape(32 * rows, feat)

        all_in = both_halves(near[:, 0], swapped[:, 0])
        all_grad = both_halves(near[:, 1], swapped[:, 1])

    sums, all_in, all_grad = lax.optimization_barrier((terms, all_in, all_grad))
    sums = sums.reshape(8, 2, 2, 2, part, hid).astype(f32).sum(axis=0)
    pre_act, back_grad = (
        sums[:, k].transpose(1, 0, 2, 3).reshape(2 * rows, hid) for k in (0, 1)
    )
    act_value, pullback = jax.vjp(gelu_tanh, pre_act)
    activation = act_value.astype(bf16)
    pre_grad = pullback(back_grad)[0].astype(bf16)
    pre_grad = lax.all_gather(pre_grad, ROW, axis_index_groups=ROW_ORDER, axis=0, tiled=True)

    with jax.named_scope("token_sum"):
        terms = dot(pre_grad, w_in, ((1,), (1,)), bf16).reshape(32, rows, feat)
        terms, activation = lax.optimization_barrier((terms, activation))
        terms = lax.all_to_all(terms, PLANE, 0, 0, tiled=True)
        grad_inputs = terms.astype(f32).sum(axis=0).astype(bf16)

    activation = lax.all_gather(activation, ROW, axis_index_groups=ROW_ORDER, axis=0, tiled=True)
    activation, pre_grad = lax.optimization_barrier((activation, pre_grad))
    grad_w_in = dot(all_in, pre_grad, ((0,), (0,)), bf16)
    grad_w_out = dot(activation, all_grad, ((0,), (0,)), bf16)
    return (grad_inputs, grad_w_in, grad_w_out)


def solution(mesh):
    fine = Mesh(mesh.devices.reshape(2, 8, 2, 4, 4), ("y_hi", "z", "core", "x", "y_lo"))
    plane = ("y_hi", "x", "y_lo")
    token_block, up_block, down_block = P(plane, ROW), P(ROW, plane), P(plane, ROW)
    return jax.shard_map(
        body,
        mesh=fine,
        in_specs=(token_block, token_block, up_block, down_block),
        out_specs=(token_block, up_block, down_block),
        check_vma=False,
    )
```

```python
import jax
import jax.numpy as jnp
from jax import lax
from jax.experimental import pallas as pl
from jax.experimental.pallas import tpu as pltpu
from jax.sharding import Mesh
from jax.sharding import PartitionSpec as P

PLANE = ("x", "y_hi", "y_lo")
SIDE = ("y_hi", "y_lo")
ROW = ("z", "core")
SWAP = [(0, 1), (1, 0)]
SIDE_ORDER = [list(range(7, -1, -1))]
ROW_ORDER = [[2 * z + core for z in range(7, -1, -1) for core in (0, 1)]]


def gelu_tanh(value):
    return jax.nn.gelu(value, approximate=True)


def dot(left, right, dims, out=jnp.float32):
    return lax.dot_general(
        left, right, (dims, ((), ())), preferred_element_type=jnp.float32
    ).astype(out)


def stage_kernel(weight, held, sem):
    copy = pltpu.make_async_copy(weight, held, sem)
    copy.start()
    copy.wait()


def stage_weight(weight):
    return pl.pallas_call(
        stage_kernel,
        in_specs=[pl.BlockSpec(memory_space=pltpu.HBM)],
        out_specs=pl.BlockSpec(memory_space=pltpu.VMEM),
        out_shape=pltpu.VMEM(weight.shape, weight.dtype),
        scratch_shapes=[pltpu.SemaphoreType.DMA],
        compiler_params=pltpu.CompilerParams(vmem_limit_bytes=8 * 1024 * 1024),
        cost_estimate=pl.CostEstimate(
            flops=0, bytes_accessed=4 * weight.size, transcendentals=0
        ),
        name="stage_weight",
    )(pltpu.with_memory_space_constraint(weight, pltpu.HBM))


def terms_kernel(core, tokens, up, down, far_up, far_down, terms, held, total, sems):
    near, far = core[0], 1 - core[0]
    share, hid = terms.shape[2:]
    feat = tokens.shape[4]
    block = 256
    fetches = [
        pltpu.make_async_copy(source, held.at[k], sems.at[k])
        for k, source in enumerate((down, far_up, far_down))
    ]
    for fetch in fetches:
        fetch.start()

    def product(side, kind, weights, span):
        left = tokens[:, side, kind].reshape(16 * share, feat)
        if kind == 0:
            return dot(left, weights[:, span], ((1,), (0,)))
        return dot(left, weights[span, :], ((1,), (1,)))

    spans = [pl.ds(j * block, block) for j in range(hid // block)]
    for span in spans:
        total[0, :, span] = product(near, 0, up, span)
    for fetch in fetches:
        fetch.wait()
    for span in spans:
        total[1, :, span] = product(near, 1, held.at[0], span)
    for kind in (0, 1):
        for span in spans:
            value = total[kind, :, span] + product(far, kind, held.at[1 + kind], span)
            terms[:, kind, :, span] = value.astype(terms.dtype).reshape(16, share, block)


def chip_terms(core, tokens, up, down, far_up, far_down):
    feat, hid = up.shape
    count = tokens.shape[0] * tokens.shape[3]
    up = pltpu.with_memory_space_constraint(up, pltpu.VMEM)
    rest = [pltpu.with_memory_space_constraint(w, pltpu.HBM) for w in (down, far_up, far_down)]
    far = pl.BlockSpec(memory_space=pltpu.HBM)
    near = pl.BlockSpec(memory_space=pltpu.VMEM)
    return pl.pallas_call(
        terms_kernel,
        in_specs=[pl.BlockSpec(memory_space=pltpu.SMEM), near, near, far, far, far],
        out_specs=near,
        out_shape=jax.ShapeDtypeStruct((16, 2, count // 16, hid), jnp.bfloat16),
        scratch_shapes=[
            pltpu.VMEM((3, feat, hid), jnp.bfloat16),
            pltpu.VMEM((2, count, hid), jnp.float32),
            pltpu.SemaphoreType.DMA((3,)),
        ],
        compiler_params=pltpu.CompilerParams(vmem_limit_bytes=32 * 1024 * 1024),
        cost_estimate=pl.CostEstimate(
            flops=8 * count * feat * hid, bytes_accessed=8 * feat * hid, transcendentals=0
        ),
        name="chip_terms",
    )(core, tokens, up, *rest)


def body(inputs, out_grad, w_in, w_out):
    bf16, f32 = jnp.bfloat16, jnp.float32
    feat, hid = w_in.shape
    rows = inputs.shape[0]
    part = rows // 2
    core = lax.axis_index("core")
    first = core == 0

    with jax.named_scope("gather_tokens"):
        own = jnp.concatenate([inputs, out_grad])
        own = jnp.broadcast_to(own[None], (8,) + own.shape)
        by_y = lax.all_to_all(own, SIDE, 0, 0, axis_index_groups=SIDE_ORDER, tiled=True)
        by_y, w_in_own, w_out_own = lax.optimization_barrier((by_y, w_in, w_out))
        by_y = by_y.reshape(8, 2, 2, part, feat)
        by_y = by_y[::-1].transpose(2, 1, 0, 3, 4).reshape(2, 2, 8 * part, feat)
        by_x = jnp.broadcast_to(by_y[None], (4,) + by_y.shape)
        by_x = by_x.reshape(8, 2, 8 * part, feat)
        by_x = lax.all_to_all(by_x, ("x", "core"), 0, 0, tiled=True)
        by_x = by_x.reshape(4, 2, 2, 8 * part, feat)
        w_in_swap = lax.ppermute(w_in_own, "core", SWAP)
        w_out_swap = lax.ppermute(w_out_own, "core", SWAP)
        near = lax.dynamic_index_in_dim(by_x, core, 1, False)
        far = lax.dynamic_index_in_dim(by_x, 1 - core, 1, False)

    with jax.named_scope("row_sum"):
        up = stage_weight(w_in_own)
        terms = chip_terms(core.reshape(1), by_x, up, w_out, w_in_swap, w_out_swap)
        terms = lax.all_to_all(terms, ROW, 0, 0, axis_index_groups=ROW_ORDER, tiled=True)

    with jax.named_scope("swap_tokens"):
        swapped = lax.ppermute(far, "core", SWAP)

        def both_halves(near, far):
            near, far = near.reshape(32, part, feat), far.reshape(32, part, feat)
            halves = [jnp.where(first, near, far), jnp.where(first, far, near)]
            return jnp.stack(halves, axis=1).reshape(32 * rows, feat)

        all_in = both_halves(near[:, 0], swapped[:, 0])
        all_grad = both_halves(near[:, 1], swapped[:, 1])

    sums, all_in, all_grad = lax.optimization_barrier((terms, all_in, all_grad))
    sums = sums.reshape(8, 2, 2, 2, part, hid).astype(f32).sum(axis=0)
    pre_act, back_grad = (
        sums[:, k].transpose(1, 0, 2, 3).reshape(2 * rows, hid) for k in (0, 1)
    )
    act_value, pullback = jax.vjp(gelu_tanh, pre_act)
    activation = act_value.astype(bf16)
    pre_grad = pullback(back_grad)[0].astype(bf16)
    pre_grad = lax.all_gather(pre_grad, ROW, axis_index_groups=ROW_ORDER, axis=0, tiled=True)

    with jax.named_scope("token_sum"):
        terms = dot(pre_grad, w_in, ((1,), (1,)), bf16).reshape(32, rows, feat)
        terms, activation = lax.optimization_barrier((terms, activation))
        terms = lax.all_to_all(terms, PLANE, 0, 0, tiled=True)
        grad_inputs = terms.astype(f32).sum(axis=0).astype(bf16)

    activation = lax.all_gather(activation, ROW, axis_index_groups=ROW_ORDER, axis=0, tiled=True)
    activation, pre_grad = lax.optimization_barrier((activation, pre_grad))
    grad_w_in = dot(all_in, pre_grad, ((0,), (0,)), bf16)
    grad_w_out = dot(activation, all_grad, ((0,), (0,)), bf16)
    return (grad_inputs, grad_w_in, grad_w_out)


def solution(mesh):
    fine = Mesh(mesh.devices.reshape(2, 8, 2, 4, 4), ("y_hi", "z", "core", "x", "y_lo"))
    plane = ("y_hi", "x", "y_lo")
    token_block, up_block, down_block = P(plane, ROW), P(ROW, plane), P(plane, ROW)
    return jax.shard_map(
        body,
        mesh=fine,
        in_specs=(token_block, token_block, up_block, down_block),
        out_specs=(token_block, up_block, down_block),
        check_vma=False,
    )
```
